256 devices in a mesh: view: 8 (over z), wide: 32 (over y, x, core).
Axes of the slice: x: 4, y: 4, z: 8, core: 2. Of those that a mesh axis runs over, the one named last changes fastest.
Arguments:
- tracer: float32 [512, 1024, 128], P('view', 'wide'), may hold values from 0.05 to 5
- velocity: float32 [3, 512, 1024, 128], P(None, 'view', 'wide'), may hold values from -0.15 to 0.15
- buildings: int32 [512, 1024, 128], P('view', 'wide'), may hold values from 0 to 1, as said below
- source: float32 [512, 1024, 128], P('view', 'wide'), may hold values from 0 to 0.5
Outputs:
- tracer_next: float32 [512, 1024, 128], P('view', 'wide')
- picture: float32 [4, 1024, 128], P(None, 'wide', 'view')
The draws below stay inside these ranges and needn't reach their ends.
Inputs may be any that keep to these rules, and one draw needn't show every extreme that they name: `buildings`: each column of cells at a fixed first and second index is inside a building from the ground up to some height of at most 64 cells, and outside above it.
All inputs are finite; a program needn't handle non-finite values.
Results may differ from the reference program's by a relative error of at most 0.000056.
Values sent between devices are 32-bit elements; how exact they have to be, the bound alone decides.
A program may use at most 64 MiB of HBM per device.

```python
import math
import jax
import jax.numpy as jnp

NZ = 128
STEPS = 4
NX = 512
NY = 1024


def draw_buildings(key, part):
    lot_key = jax.random.fold_in(key, 11)
    tall_key = jax.random.fold_in(key, 23)
    built_lots = jax.random.randint(lot_key, (NX, NY), 0, 2)
    height_draw = jax.random.randint(tall_key, (NX, NY), 1, NZ // 2 + 1)
    heights = (built_lots * height_draw).astype(jnp.int32)
    heights = heights.at[0, 0].set(NZ // 2)
    levels = jnp.arange(NZ, dtype=jnp.int32)
    return (levels[None, None, :] < heights[:, :, None]).astype(jnp.int32)


def draw_velocity(key, part):
    size_key = jax.random.fold_in(key, 31)
    first_key = jax.random.fold_in(key, 37)
    second_key = jax.random.fold_in(key, 41)
    third_key = jax.random.fold_in(key, 43)
    flip_first_key = jax.random.fold_in(key, 47)
    flip_second_key = jax.random.fold_in(key, 53)
    spread = jax.random.uniform(size_key, (3, NX, NY, NZ), jnp.float32, 0.0, math.log(2.0))
    magnitude = 0.15 * jnp.exp(-spread)
    column_first = jax.random.randint(first_key, (1, 1, NY, NZ), 0, 2) * 2 - 1
    flips_first = jnp.where(jax.random.randint(flip_first_key, (1, NX, NY, NZ), 0, 16) == 0, -1, 1)
    column_second = jax.random.randint(second_key, (1, NX, 1, NZ), 0, 2) * 2 - 1
    flips_second = jnp.where(jax.random.randint(flip_second_key, (1, NX, NY, NZ), 0, 16) == 0, -1, 1)
    sign_third = jax.random.randint(third_key, (1, NX, NY, NZ), 0, 2) * 2 - 1
    sign_first = (column_first * flips_first).astype(jnp.float32)
    sign_second = (column_second * flips_second).astype(jnp.float32)
    signs = jnp.concatenate([sign_first, sign_second, sign_third.astype(jnp.float32)], axis=0)
    return (magnitude * signs).astype(jnp.float32)


def block_levels(stream_key, dims, pieces, smallest, high):
    factor_of, own = 1.0, jax.random.fold_in(stream_key, 6)
    for position, shards_of in pieces:
        steps = jnp.exp(jax.random.uniform(jax.random.fold_in(own, position), (shards_of,), jnp.float32, smallest / len(pieces), high / len(pieces)))
        factor_of = factor_of * jnp.repeat(steps, dims[position] // shards_of).reshape([-1 if axis == position else 1 for axis in range(len(dims))])
    return factor_of


def setup_inputs(seed: int = 0) -> dict:
    seeds = jax.random.split(jax.random.key(seed), 5)
    return {
        "tracer": jnp.clip(jnp.exp(math.log(5.0) - 4.6051702 * jax.random.uniform(seeds[0], (NX, NY, NZ), jnp.float32) ** block_levels(seeds[0], (NX, NY, NZ), ((0, 8), (1, 32)), -0.2, 0.2)), 0.05, 5.0),
        "velocity": draw_velocity(jax.random.fold_in(seeds[4], 71), 0),
        "buildings": draw_buildings(jax.random.fold_in(seeds[4], 71), 0),
        "source": jnp.clip(0.5 * jax.random.uniform(seeds[3], (NX, NY, NZ), jnp.float32) ** block_levels(seeds[3], (NX, NY, NZ), ((0, 8), (1, 32)), -0.2, 0.2), 0.0, 0.5),
    }


def advance(tracer, velocity, open_cells, source):
    face_zero = velocity[0][:-1] * open_cells[:-1] * open_cells[1:]
    flux_zero = jnp.maximum(face_zero, 0.0) * tracer[:-1] + jnp.minimum(face_zero, 0.0) * tracer[1:]
    delta_zero = (flux_zero[1:] - flux_zero[:-1])[:, 1:-1]
    face_one = velocity[1][:, :-1] * open_cells[:, :-1] * open_cells[:, 1:]
    flux_one = jnp.maximum(face_one, 0.0) * tracer[:, :-1] + jnp.minimum(face_one, 0.0) * tracer[:, 1:]
    delta_one = (flux_one[:, 1:] - flux_one[:, :-1])[1:-1]
    face_two = velocity[2][:, :, :-1] * open_cells[:, :, :-1] * open_cells[:, :, 1:]
    flux_two = jnp.maximum(face_two, 0.0) * tracer[:, :, :-1] + jnp.minimum(face_two, 0.0) * tracer[:, :, 1:]
    padded = jnp.pad(flux_two, ((0, 0), (0, 0), (1, 1)))
    delta_two = (padded[:, :, 1:] - padded[:, :, :-1])[1:-1, 1:-1]
    inner_tracer = tracer[1:-1, 1:-1]
    return open_cells[1:-1, 1:-1] * (inner_tracer - delta_zero - delta_one - delta_two + source[1:-1, 1:-1])


def shade_cells(tracer, open_cells):
    shading = tracer / (1.0 + tracer)
    walls = 1.0 - open_cells
    red = open_cells * shading + 0.55 * walls
    green = open_cells * jnp.exp(-0.5 * tracer) + 0.5 * walls
    blue = open_cells * (0.2 + 0.6 * shading * shading) + 0.45 * walls
    return red, green, blue


def extinction_of(tracer, open_cells, depth_cells):
    return (tracer * open_cells + 4.0 * (1.0 - open_cells)) / depth_cells


def pad_wrap(field):
    return jnp.pad(field, ((1, 1), (1, 1), (0, 0)), mode="wrap")


def reference(tracer, velocity, buildings, source):
    open_cells = (1 - buildings).astype(jnp.float32)
    open_wide = pad_wrap(open_cells)
    source_wide = pad_wrap(source)
    velocity_wide = jnp.pad(velocity, ((0, 0), (1, 1), (1, 1), (0, 0)), mode="wrap")
    current = tracer
    for substep in range(STEPS):
        current = advance(pad_wrap(current), velocity_wide, open_wide, source_wide)
    extinction = extinction_of(current, open_cells, NX * 1.0)
    before = jnp.cumsum(extinction, axis=0) - extinction
    weight = jnp.exp(-before) * (1.0 - jnp.exp(-extinction))
    red, green, blue = shade_cells(current, open_cells)
    picture = jnp.stack([jnp.sum(weight * red, axis=0), jnp.sum(weight * green, axis=0), jnp.sum(weight * blue, axis=0), 1.0 - jnp.exp(-jnp.sum(extinction, axis=0))])
    return current, picture
```

```python
import functools
import math

import jax
import jax.numpy as jnp
from jax import lax
from jax.experimental import pallas as pl
from jax.experimental.pallas import tpu as pltpu
from jax.sharding import PartitionSpec as P

STEPS = 4
H = STEPS
Y0 = 8
MESH = pl.DeviceIdType.MESH
LOG2E = math.log2(math.e)
UNROLL = 8


def sweep(start, count, body, carry, unroll=UNROLL):
    trips = count // unroll

    def chunk(trip, carry):
        first = start + trip * unroll
        for offset in range(unroll):
            carry = body(first + offset, carry)
        return carry

    if trips > 1:
        carry = lax.fori_loop(0, trips, chunk, carry)
    elif trips == 1:
        carry = chunk(0, carry)
    for offset in range(trips * unroll, count):
        carry = body(start + offset, carry)
    return carry


def flux(speed, lower, upper):
    return jnp.where(speed > 0.0, lower, upper) * speed


def face_range(side, size, depth):
    if side == 0:
        return 0, 0, size
    if side > 0:
        return size - depth, -depth, depth
    return 0, size, depth


def kernel(
    nx, ny, nz, views, wides,
    tracer, velocity, buildings, source,
    out, picture,
    t_raw, v_raw, b_raw, s_raw, wx, wy, wz, src, c0, c1, c2, c3, c4,
    acc, mid_acc, part, pieces,
    local_sem, out_sem, send_sem, recv_sem, piece_send, piece_recv,
):
    my_view, my_wide = lax.axis_index("view"), lax.axis_index("wide")

    def device(dv, dw):
        return (lax.rem(my_view + dv + views, views), lax.rem(my_wide + dw + wides, wides))

    neighbours = [(dv, dw) for dv in (0, 1, -1) for dw in (0, 1, -1) if (dv, dw) != (0, 0)]
    far = [(dv, 0) for dv in range(2, views - 1)]

    own_planes, own_rows = pl.ds(H + 1, nx), pl.ds(Y0, ny)
    loads = [
        pltpu.make_async_copy(buildings, b_raw.at[own_planes, own_rows], local_sem.at[0]),
        pltpu.make_async_copy(velocity, v_raw.at[:, own_planes, own_rows], local_sem.at[1]),
        pltpu.make_async_copy(tracer, t_raw.at[own_planes, own_rows], local_sem.at[2]),
        pltpu.make_async_copy(source, s_raw.at[own_planes, own_rows], local_sem.at[3]),
    ]
    for load in loads:
        load.start()

    barrier = pltpu.get_barrier_semaphore()
    for dv, dw in neighbours + far:
        pl.semaphore_signal(barrier, inc=1, device_id=device(dv, dw), device_id_type=MESH)
    pl.semaphore_wait(barrier, len(neighbours) + len(far))

    sends = []

    def send(ref, buffer, dv, dw, depth, pick=None):
        xs, xd, xn = face_range(dv, nx, depth)
        ys, yd, yn = face_range(dw, ny, depth)
        here = (pl.ds(xs, xn), pl.ds(ys, yn))
        there = (pl.ds(xd + H + 1, xn), pl.ds(yd + Y0, yn))
        if pick is not None:
            here, there = (pick,) + here, (pick,) + there
        index = len(sends)
        copy = pltpu.make_async_remote_copy(
            src_ref=ref.at[here], dst_ref=buffer.at[there],
            send_sem=send_sem.at[index], recv_sem=recv_sem.at[index],
            device_id=device(dv, dw), device_id_type=MESH,
        )
        copy.start()
        sends.append(copy)

    for dv, dw in sorted(neighbours, key=lambda n: -abs(n[0]) - 2 * abs(n[0] * n[1])):
        corner = dv != 0 and dw != 0
        send(buildings, b_raw, dv, dw, H - 1 if corner else H)
        send(tracer, t_raw, dv, dw, H - 1 if corner else H)
        if (dv, dw) == (1, 0):
            send(velocity, v_raw, dv, dw, H, pl.ds(0, 1))
            send(velocity, v_raw, dv, dw, H - 1, pl.ds(1, 2))
        elif (dv, dw) == (0, 1):
            send(velocity, v_raw, dv, dw, H, pl.ds(1, 1))
            send(velocity, v_raw, dv, dw, H - 1, pl.ds(0, 1))
            send(velocity, v_raw, dv, dw, H - 1, pl.ds(2, 1))
        else:
            send(velocity, v_raw, dv, dw, H - 1, pl.ds(0, 3))
        send(source, s_raw, dv, dw, H - 2 if corner else H - 1)

    levels = (c0, c1, c2, c3, c4)
    below_top = lax.broadcasted_iota(jnp.int32, (1, nz), 1) < nz - 1

    def prepare(first, count, row, rows, shift):
        here, up = pl.ds(row, rows), pl.ds(row + 1, rows)

        def body(p, b_here):
            b_next = b_raw[p + 1, here, :]
            b_up = pltpu.roll(b_here, rows - 1, 0) if shift == "roll" else b_raw[p, up, :]
            open_here = b_here == 0
            wx[p, here, :] = jnp.where((b_here | b_next) == 0, v_raw[0, p, here, :], 0.0)
            wy[p, here, :] = jnp.where((b_here | b_up) == 0, v_raw[1, p, here, :], 0.0)
            wz[p, here, :] = jnp.where(open_here & below_top, v_raw[2, p, here, :], 0.0)
            src[p, here, :] = jnp.where(open_here, s_raw[p, here, :], 0.0)
            c0[p, here, :] = jnp.where(open_here, t_raw[p, here, :], 0.0)
            return b_next

        sweep(first, count, body, b_raw[first, here, :])

    def advance(step, first, count, row, rows, shift, shade=None, carry=()):
        old, new = levels[step - 1], levels[step]
        here, up, low = pl.ds(row, rows), pl.ds(row + 1, rows), pl.ds(row - 1, rows)

        def body(p, state):
            here_c, flux_low, carry = state
            next_c = old[p + 1, here, :]
            flux_x = flux(wx[p, here, :], here_c, next_c)
            wy_here = wy[p, here, :]
            if shift == "roll":
                flux_y = flux(wy_here, here_c, pltpu.roll(here_c, rows - 1, 0))
                flux_y_low = pltpu.roll(flux_y, 1, 0)
            else:
                flux_y = flux(wy_here, here_c, old[p, up, :])
                flux_y_low = flux(wy[p, low, :], old[p, low, :], here_c)
            flux_z = flux(wz[p, here, :], here_c, pltpu.roll(here_c, nz - 1, 1))
            flux_z_low = pltpu.roll(flux_z, 1, 1)
            value = here_c + src[p, here, :] - (flux_x - flux_low) - (flux_y - flux_y_low) - (flux_z - flux_z_low)
            new[p, here, :] = value
            if shade is not None:
                carry = shade(value, b_raw[p, here, :], carry)
            return next_c, flux_x, carry

        here_c = old[first, here, :]
        flux_low = flux(wx[first - 1, here, :], old[first - 1, here, :], here_c)
        return sweep(first, count, body, (here_c, flux_low, carry))[2]

    scale = LOG2E / (nx * views)

    def shade(value, built, carry):
        depth, through, red, green, blue = carry
        wall = built != 0
        depth = depth + jnp.where(wall, 4.0, value) * scale
        after = jnp.exp2(-depth)
        weight = through - after
        shading = value / (1.0 + value)
        red = red + weight * jnp.where(wall, 0.55, shading)
        green = green + weight * jnp.where(wall, 0.5, jnp.exp2(value * (-0.5 * LOG2E)))
        blue = blue + weight * jnp.where(wall, 0.45, 0.2 + 0.6 * (shading * shading))
        return depth, after, red, green, blue

    def nothing(rows):
        zero = jnp.zeros((rows, nz), jnp.float32)
        return zero, jnp.ones((rows, nz), jnp.float32), zero, zero, zero

    x0 = H + 1
    for load in loads:
        load.wait()
    prepare(x0, nx - 1, Y0, ny, "roll")
    last = x0 + nx - 1
    c0[last, own_rows, :] = jnp.where(b_raw[last, own_rows, :] == 0, t_raw[last, own_rows, :], 0.0)
    for step in range(1, STEPS):
        advance(step, x0 + step, nx - 2 * step, Y0, ny, "roll")
    middle = ny - 2 * H
    carry = advance(STEPS, x0 + STEPS, nx - 2 * STEPS, Y0 + H, middle, "load", shade, nothing(middle))
    for i in range(5):
        mid_acc[i] = carry[i]

    for copy in sends:
        copy.wait_recv()
    y_first, wide_rows = Y0 - H, ny + 2 * H
    prepare(1, H, y_first, wide_rows, "load")
    prepare(x0 + nx - 1, H + 1, y_first, wide_rows, "load")
    edges = ((Y0 - H, 2 * H), (Y0 + ny - H, 2 * H))
    for row, rows in edges:
        prepare(x0, nx - 1, row, rows, "load")
    for step in range(1, STEPS):
        advance(step, x0 - H + step, H, y_first, wide_rows, "load")
        for row, rows in edges:
            advance(step, x0 + step, nx - 2 * step, row, rows, "load")
        advance(step, x0 + nx - step, H, y_first, wide_rows, "load")
    carry = advance(STEPS, x0, H, y_first, wide_rows, "load", shade, nothing(wide_rows))
    for i in range(5):
        acc[i] = carry[i]
    for row, rows in edges:
        carry = tuple(acc[i, row - y_first:row - y_first + rows] for i in range(5))
        carry = advance(STEPS, x0 + H, nx - 2 * H, row, rows, "load", shade, carry)
        for i in range(5):
            acc[i, row - y_first:row - y_first + rows] = carry[i]
    inner = slice(2 * H, 2 * H + middle)
    front = acc[1, inner]
    for i in (2, 3, 4):
        acc[i, inner] = acc[i, inner] + front * mid_acc[i]
    depth = acc[0, inner] + mid_acc[0]
    acc[0, inner] = depth
    acc[1, inner] = jnp.exp2(-depth)
    carry = tuple(acc[i] for i in range(5))
    carry = advance(STEPS, x0 + nx - H, H, y_first, wide_rows, "load", shade, carry)
    for i in range(5):
        acc[i] = carry[i]

    store = pltpu.make_async_copy(c4.at[own_planes, own_rows], out, out_sem)
    store.start()

    stacked = jnp.concatenate([acc[i, H:H + ny] for i in (2, 3, 4, 1)], axis=0)
    part[...] = stacked.T
    share = nz // views
    copies = []
    for hop in range(1, views):
        target = lax.rem(my_view + hop, views)
        copy = pltpu.make_async_remote_copy(
            src_ref=part.at[pl.ds(pl.multiple_of(target * share, share), share)],
            dst_ref=pieces.at[my_view],
            send_sem=piece_send.at[hop - 1], recv_sem=piece_recv.at[hop - 1],
            device_id=device(hop, 0), device_id_type=MESH,
        )
        copy.start()
        copies.append(copy)
    pieces[my_view] = part[pl.ds(pl.multiple_of(my_view * share, share), share), :]
    for copy in copies:
        copy.wait_recv()
    lane = lax.broadcasted_iota(jnp.int32, (share, 4 * ny), 1)
    colors = jnp.zeros((share, 4 * ny), jnp.float32)
    through = jnp.ones((share, 4 * ny), jnp.float32)
    for brick in range(views):
        piece = pieces[brick]
        spread = piece
        for group in range(3):
            turned = pltpu.roll(piece, (group + 1) * ny, 1)
            spread = jnp.where(lane // ny == group, turned, spread)
        colors = colors + through * piece
        through = through * spread
    pixels = jnp.where(lane < 3 * ny, colors, 1.0 - through)
    for i in range(4):
        picture[i] = pixels[:, i * ny:(i + 1) * ny]

    for copy in sends + copies:
        copy.wait_send()
    store.wait()


def on_device(tracer, velocity, buildings, source):
    nx, ny, nz = tracer.shape
    views, wides = lax.axis_size("view"), lax.axis_size("wide")
    field = (nx + 2 * H + 2, ny + 2 * Y0, nz)
    buffer = pltpu.VMEM(field, jnp.float32)
    n_sends = 40
    tracer_next, picture = pl.pallas_call(
        functools.partial(kernel, nx, ny, nz, views, wides),
        out_shape=(
            jax.ShapeDtypeStruct((nx, ny, nz), jnp.float32),
            jax.ShapeDtypeStruct((4, nz // views, ny), jnp.float32),
        ),
        in_specs=[pl.BlockSpec(memory_space=pltpu.HBM)] * 4,
        out_specs=(pl.BlockSpec(memory_space=pltpu.HBM), pl.BlockSpec(memory_space=pltpu.VMEM)),
        scratch_shapes=[
            buffer,
            pltpu.VMEM((3,) + field, jnp.float32),
            pltpu.VMEM(field, jnp.int32),
        ]
        + [buffer] * 10
        + [
            pltpu.VMEM((5, ny + 2 * H, nz), jnp.float32),
            pltpu.VMEM((5, ny - 2 * H, nz), jnp.float32),
            pltpu.VMEM((nz, 4 * ny), jnp.float32),
            pltpu.VMEM((views, nz // views, 4 * ny), jnp.float32),
            pltpu.SemaphoreType.DMA((4,)),
            pltpu.SemaphoreType.DMA,
            pltpu.SemaphoreType.DMA((n_sends,)),
            pltpu.SemaphoreType.DMA((n_sends,)),
            pltpu.SemaphoreType.DMA((views - 1,)),
            pltpu.SemaphoreType.DMA((views - 1,)),
        ],
        compiler_params=pltpu.CompilerParams(
            collective_id=0, has_side_effects=True, vmem_limit_bytes=60 * 1024 * 1024
        ),
    )(tracer, velocity, buildings, source)
    return tracer_next, jnp.swapaxes(picture, 1, 2)


def solution(mesh):
    return jax.shard_map(
        on_device,
        mesh=mesh,
        in_specs=(
            P("view", "wide", None),
            P(None, "view", "wide", None),
            P("view", "wide", None),
            P("view", "wide", None),
        ),
        out_specs=(P("view", "wide", None), P(None, "wide", "view")),
        check_vma=False,
    )
```

```python
import functools
import math

import jax
import jax.numpy as jnp
from jax import lax
from jax.experimental import pallas as pl
from jax.experimental.pallas import tpu as pltpu
from jax.sharding import PartitionSpec as P

STEPS = 4
H = STEPS
Y0 = 8
MESH = pl.DeviceIdType.MESH
LOG2E = math.log2(math.e)


def sweep(start, count, unroll, body, carry):
    trips = count // unroll

    def chunk(trip, carry):
        first = start + trip * unroll
        for offset in range(unroll):
            carry = body(first + offset, carry)
        return carry

    if trips > 1:
        carry = lax.fori_loop(0, trips, chunk, carry)
    elif trips == 1:
        carry = chunk(0, carry)
    for offset in range(trips * unroll, count):
        carry = body(start + offset, carry)
    return carry


def flux(speed, lower, upper):
    return jnp.where(speed > 0.0, lower, upper) * speed


def face_range(side, size, depth):
    if side == 0:
        return 0, 0, size
    if side > 0:
        return size - depth, -depth, depth
    return 0, size, depth


def kernel(
    nx, ny, nz, views, wides,
    tracer, velocity, buildings, source,
    out, picture,
    t_raw, v_raw, b_raw, s_raw, wx, wy, wz, src, c0, c1, c2, c3, c4,
    acc, mid_acc, part, pieces,
    local_sem, out_sem, send_sem, recv_sem, piece_send, piece_recv,
):
    my_view, my_wide = lax.axis_index("view"), lax.axis_index("wide")

    def device(dv, dw):
        return (lax.rem(my_view + dv + views, views), lax.rem(my_wide + dw + wides, wides))

    neighbours = [(dv, dw) for dv in (0, 1, -1) for dw in (0, 1, -1) if (dv, dw) != (0, 0)]
    far = [(dv, 0) for dv in range(2, views - 1)]

    own_planes, own_rows = pl.ds(H + 1, nx), pl.ds(Y0, ny)
    loads = [
        pltpu.make_async_copy(buildings, b_raw.at[own_planes, own_rows], local_sem.at[0]),
        pltpu.make_async_copy(velocity, v_raw.at[:, own_planes, own_rows], local_sem.at[1]),
        pltpu.make_async_copy(tracer, t_raw.at[own_planes, own_rows], local_sem.at[2]),
        pltpu.make_async_copy(source, s_raw.at[own_planes, own_rows], local_sem.at[3]),
    ]
    for load in loads:
        load.start()

    barrier = pltpu.get_barrier_semaphore()
    for dv, dw in neighbours + far:
        pl.semaphore_signal(barrier, inc=1, device_id=device(dv, dw), device_id_type=MESH)
    pl.semaphore_wait(barrier, len(neighbours) + len(far))

    sends = []

    def send(ref, buffer, dv, dw, depth, pick=None):
        xs, xd, xn = face_range(dv, nx, depth)
        ys, yd, yn = face_range(dw, ny, depth)
        here = (pl.ds(xs, xn), pl.ds(ys, yn))
        there = (pl.ds(xd + H + 1, xn), pl.ds(yd + Y0, yn))
        if pick is not None:
            here, there = (pick,) + here, (pick,) + there
        index = len(sends)
        copy = pltpu.make_async_remote_copy(
            src_ref=ref.at[here], dst_ref=buffer.at[there],
            send_sem=send_sem.at[index], recv_sem=recv_sem.at[index],
            device_id=device(dv, dw), device_id_type=MESH,
        )
        copy.start()
        sends.append(copy)

    for dv, dw in sorted(neighbours, key=lambda n: -abs(n[0]) - 2 * abs(n[0] * n[1])):
        corner = dv != 0 and dw != 0
        send(buildings, b_raw, dv, dw, H - 1 if corner else H)
        send(tracer, t_raw, dv, dw, H - 1 if corner else H)
        if (dv, dw) == (1, 0):
            send(velocity, v_raw, dv, dw, H, pl.ds(0, 1))
            send(velocity, v_raw, dv, dw, H - 1, pl.ds(1, 2))
        elif (dv, dw) == (0, 1):
            send(velocity, v_raw, dv, dw, H, pl.ds(1, 1))
            send(velocity, v_raw, dv, dw, H - 1, pl.ds(0, 1))
            send(velocity, v_raw, dv, dw, H - 1, pl.ds(2, 1))
        else:
            send(velocity, v_raw, dv, dw, H - 1, pl.ds(0, 3))
        send(source, s_raw, dv, dw, H - 2 if corner else H - 1)

    levels = (c0, c1, c2, c3, c4)
    below_top = lax.broadcasted_iota(jnp.int32, (1, nz), 1) < nz - 1

    def prepare(first, count, windows, unroll, shift="load"):
        def body(p, built):
            return tuple(cells(p, row, rows, b_here) for (row, rows), b_here in zip(windows, built))

        def cells(p, row, rows, b_here):
            here = pl.ds(row, rows)
            b_next = b_raw[p + 1, here, :]
            b_up = pltpu.roll(b_here, rows - 1, 0) if shift == "roll" else b_raw[p, pl.ds(row + 1, rows), :]
            open_here = b_here == 0
            wx[p, here, :] = jnp.where((b_here | b_next) == 0, v_raw[0, p, here, :], 0.0)
            wy[p, here, :] = jnp.where((b_here | b_up) == 0, v_raw[1, p, here, :], 0.0)
            wz[p, here, :] = jnp.where(open_here & below_top, v_raw[2, p, here, :], 0.0)
            src[p, here, :] = jnp.where(open_here, s_raw[p, here, :], 0.0)
            c0[p, here, :] = jnp.where(open_here, t_raw[p, here, :], 0.0)
            return b_next

        sweep(first, count, unroll, body, tuple(b_raw[first, pl.ds(row, rows), :] for row, rows in windows))

    def advance(step, first, count, windows, unroll, shift="load", shade=None, carries=None):
        old, new = levels[step - 1], levels[step]

        def body(p, states):
            return tuple(cells(p, row, rows, state) for (row, rows), state in zip(windows, states))

        def cells(p, row, rows, state):
            here_c, flux_low, carry = state
            here, up, low = pl.ds(row, rows), pl.ds(row + 1, rows), pl.ds(row - 1, rows)
            next_c = old[p + 1, here, :]
            flux_x = flux(wx[p, here, :], here_c, next_c)
            wy_here = wy[p, here, :]
            if shift == "roll":
                flux_y = flux(wy_here, here_c, pltpu.roll(here_c, rows - 1, 0))
                flux_y_low = pltpu.roll(flux_y, 1, 0)
            else:
                flux_y = flux(wy_here, here_c, old[p, up, :])
                flux_y_low = flux(wy[p, low, :], old[p, low, :], here_c)
            flux_z = flux(wz[p, here, :], here_c, pltpu.roll(here_c, nz - 1, 1))
            flux_z_low = pltpu.roll(flux_z, 1, 1)
            value = here_c + src[p, here, :] - (flux_x - flux_low) - (flux_y - flux_y_low) - (flux_z - flux_z_low)
            new[p, here, :] = value
            if shade is not None:
                carry = shade(value, b_raw[p, here, :], carry)
            return next_c, flux_x, carry

        states = []
        for i, (row, rows) in enumerate(windows):
            here = pl.ds(row, rows)
            here_c = old[first, here, :]
            flux_low = flux(wx[first - 1, here, :], old[first - 1, here, :], here_c)
            states.append((here_c, flux_low, carries[i] if carries else ()))
        return tuple(state[2] for state in sweep(first, count, unroll, body, tuple(states)))

    scale = LOG2E / (nx * views)

    def shade(value, built, carry):
        depth, through, red, green, blue = carry
        wall = built != 0
        depth = depth + jnp.where(wall, 4.0, value) * scale
        after = jnp.exp2(-depth)
        weight = through - after
        shading = value / (1.0 + value)
        red = red + weight * jnp.where(wall, 0.55, shading)
        green = green + weight * jnp.where(wall, 0.5, jnp.exp2(value * (-0.5 * LOG2E)))
        blue = blue + weight * jnp.where(wall, 0.45, 0.2 + 0.6 * (shading * shading))
        return depth, after, red, green, blue

    def nothing(rows):
        zero = jnp.zeros((rows, nz), jnp.float32)
        return zero, jnp.ones((rows, nz), jnp.float32), zero, zero, zero

    x0 = H + 1
    last = x0 + nx - 1
    for load in loads:
        load.wait()
    own, middle = [(Y0, ny)], [(Y0 + H, ny - 2 * H)]
    prepare(x0, nx - 1, own, 8, "roll")
    c0[last, own_rows, :] = jnp.where(b_raw[last, own_rows, :] == 0, t_raw[last, own_rows, :], 0.0)
    for step in range(1, STEPS):
        advance(step, x0 + step, nx - 2 * step, own, 8, "roll")
    centre = advance(STEPS, x0 + H, nx - 2 * H, middle, 8, "load", shade, [nothing(ny - 2 * H)])[0]
    for i in range(5):
        mid_acc[i] = centre[i]

    for copy in sends:
        copy.wait_recv()
    edges = [(Y0 - H, 2 * H), (Y0 + ny - H, 2 * H)]
    prepare(1, nx + 2 * H, edges, 24)
    prepare(1, H, middle, H)
    prepare(last, H + 1, middle, H + 1)
    for step in range(1, STEPS):
        advance(step, x0 - H + step, nx + 2 * H - 2 * step, edges, 28)
        advance(step, x0 - H + step, H, middle, H)
        advance(step, x0 + nx - step, H, middle, H)
    left, right = advance(STEPS, x0, nx, edges, 16, "load", shade, [nothing(2 * H)] * 2)
    front = advance(STEPS, x0, H, middle, H, "load", shade, [nothing(ny - 2 * H)])[0]
    depth = front[0] + mid_acc[0]
    centre = (depth, jnp.exp2(-depth)) + tuple(front[i] + front[1] * mid_acc[i] for i in (2, 3, 4))
    centre = advance(STEPS, x0 + nx - H, H, middle, H, "load", shade, [centre])[0]
    for i in range(5):
        acc[i, 0:2 * H] = left[i]
        acc[i, 2 * H:ny] = centre[i]
        acc[i, ny:ny + 2 * H] = right[i]

    store = pltpu.make_async_copy(c4.at[own_planes, own_rows], out, out_sem)
    store.start()

    stacked = jnp.concatenate([acc[i, H:H + ny] for i in (2, 3, 4, 1)], axis=0)
    part[...] = stacked.T
    share = nz // views
    copies = []
    for hop in range(1, views):
        target = lax.rem(my_view + hop, views)
        copy = pltpu.make_async_remote_copy(
            src_ref=part.at[pl.ds(pl.multiple_of(target * share, share), share)],
            dst_ref=pieces.at[my_view],
            send_sem=piece_send.at[hop - 1], recv_sem=piece_recv.at[hop - 1],
            device_id=device(hop, 0), device_id_type=MESH,
        )
        copy.start()
        copies.append(copy)
    pieces[my_view] = part[pl.ds(pl.multiple_of(my_view * share, share), share), :]
    for copy in copies:
        copy.wait_recv()
    lane = lax.broadcasted_iota(jnp.int32, (share, 4 * ny), 1)
    colors = jnp.zeros((share, 4 * ny), jnp.float32)
    through = jnp.ones((share, 4 * ny), jnp.float32)
    for brick in range(views):
        piece = pieces[brick]
        spread = piece
        for group in range(3):
            turned = pltpu.roll(piece, (group + 1) * ny, 1)
            spread = jnp.where(lane // ny == group, turned, spread)
        colors = colors + through * piece
        through = through * spread
    pixels = jnp.where(lane < 3 * ny, colors, 1.0 - through)
    for i in range(4):
        picture[i] = pixels[:, i * ny:(i + 1) * ny]

    for copy in sends + copies:
        copy.wait_send()
    store.wait()


def on_device(tracer, velocity, buildings, source):
    nx, ny, nz = tracer.shape
    views, wides = lax.axis_size("view"), lax.axis_size("wide")
    field = (nx + 2 * H + 2, ny + 2 * Y0, nz)
    buffer = pltpu.VMEM(field, jnp.float32)
    n_sends = 40
    tracer_next, picture = pl.pallas_call(
        functools.partial(kernel, nx, ny, nz, views, wides),
        out_shape=(
            jax.ShapeDtypeStruct((nx, ny, nz), jnp.float32),
            jax.ShapeDtypeStruct((4, nz // views, ny), jnp.float32),
        ),
        in_specs=[pl.BlockSpec(memory_space=pltpu.HBM)] * 4,
        out_specs=(pl.BlockSpec(memory_space=pltpu.HBM), pl.BlockSpec(memory_space=pltpu.VMEM)),
        scratch_shapes=[
            buffer,
            pltpu.VMEM((3,) + field, jnp.float32),
            pltpu.VMEM(field, jnp.int32),
        ]
        + [buffer] * 10
        + [
            pltpu.VMEM((5, ny + 2 * H, nz), jnp.float32),
            pltpu.VMEM((5, ny - 2 * H, nz), jnp.float32),
            pltpu.VMEM((nz, 4 * ny), jnp.float32),
            pltpu.VMEM((views, nz // views, 4 * ny), jnp.float32),
            pltpu.SemaphoreType.DMA((4,)),
            pltpu.SemaphoreType.DMA,
            pltpu.SemaphoreType.DMA((n_sends,)),
            pltpu.SemaphoreType.DMA((n_sends,)),
            pltpu.SemaphoreType.DMA((views - 1,)),
            pltpu.SemaphoreType.DMA((views - 1,)),
        ],
        compiler_params=pltpu.CompilerParams(
            collective_id=0, has_side_effects=True, vmem_limit_bytes=60 * 1024 * 1024
        ),
    )(tracer, velocity, buildings, source)
    return tracer_next, jnp.swapaxes(picture, 1, 2)


def solution(mesh):
    return jax.shard_map(
        on_device,
        mesh=mesh,
        in_specs=(
            P("view", "wide", None),
            P(None, "view", "wide", None),
            P("view", "wide", None),
            P("view", "wide", None),
        ),
        out_specs=(P("view", "wide", None), P(None, "wide", "view")),
        check_vma=False,
    )
```

```python
import functools
import math

import jax
import jax.numpy as jnp
from jax import lax
from jax.experimental import pallas as pl
from jax.experimental.pallas import tpu as pltpu
from jax.sharding import PartitionSpec as P

STEPS = 4
H = STEPS
Y0 = 8
MESH = pl.DeviceIdType.MESH
LOG2E = math.log2(math.e)


def sweep(start, count, unroll, body, carry):
    trips = count // unroll

    def chunk(trip, carry):
        first = start + trip * unroll
        for offset in range(unroll):
            carry = body(first + offset, carry)
        return carry

    if trips > 1:
        carry = lax.fori_loop(0, trips, chunk, carry)
    elif trips == 1:
        carry = chunk(0, carry)
    for offset in range(trips * unroll, count):
        carry = body(start + offset, carry)
    return carry


def flux(speed, lower, upper):
    return jnp.where(speed > 0.0, lower, upper) * speed


def face_range(side, size, depth):
    if side == 0:
        return 0, 0, size
    if side > 0:
        return size - depth, -depth, depth
    return 0, size, depth


def kernel(
    nx, ny, nz, views, wides,
    tracer, velocity, buildings, source,
    out, picture,
    t_raw, v_raw, b_raw, s_raw, wx, wy, wz, src, c0, c1, c2, c3, c4,
    acc, mid_acc, part, pieces,
    local_sem, out_sem, known_sem, send_sem, recv_sem, piece_send, piece_recv,
):
    my_view, my_wide = lax.axis_index("view"), lax.axis_index("wide")

    def device(dv, dw):
        return (lax.rem(my_view + dv + views, views), lax.rem(my_wide + dw + wides, wides))

    near = [(1, 0), (-1, 0), (0, 1), (0, -1)]
    corners = [(dv, dw) for dv in (1, -1) for dw in (1, -1)]

    own_planes, own_rows = pl.ds(H + 1, nx), pl.ds(Y0, ny)
    loads = [
        pltpu.make_async_copy(buildings, b_raw, local_sem.at[0]),
        pltpu.make_async_copy(tracer, t_raw, local_sem.at[1]),
        pltpu.make_async_copy(velocity, v_raw.at[:, own_planes, own_rows], local_sem.at[2]),
        pltpu.make_async_copy(source, s_raw.at[own_planes, own_rows], local_sem.at[3]),
    ]
    for load in loads:
        load.start()

    barrier = pltpu.get_barrier_semaphore()
    for dv, dw in near:
        pl.semaphore_signal(barrier, inc=1, device_id=device(dv, dw), device_id_type=MESH)
    pl.semaphore_wait(barrier, len(near))

    def tell(ring, sides):
        for dv, dw in sides:
            pl.semaphore_signal(known_sem.at[ring], inc=1, device_id=device(dv, dw), device_id_type=MESH)

    sends = []

    def send(ref, buffer, dv, dw, depth, pick=None):
        xs, xd, xn = face_range(dv, nx, depth)
        ys, yd, yn = face_range(dw, ny, depth)
        here = (pl.ds(xs, xn), pl.ds(ys, yn))
        there = (pl.ds(xd + H + 1, xn), pl.ds(yd + Y0, yn))
        if pick is not None:
            here, there = (pick,) + here, (pick,) + there
        index = len(sends)
        copy = pltpu.make_async_remote_copy(
            src_ref=ref.at[here], dst_ref=buffer.at[there],
            send_sem=send_sem.at[index], recv_sem=recv_sem.at[index],
            device_id=device(dv, dw), device_id_type=MESH,
        )
        copy.start()
        sends.append(copy)

    def send_inputs(dv, dw):
        if (dv, dw) == (1, 0):
            send(velocity, v_raw, dv, dw, H, pl.ds(0, 1))
            send(velocity, v_raw, dv, dw, H - 1, pl.ds(1, 2))
        elif (dv, dw) == (0, 1):
            send(velocity, v_raw, dv, dw, H, pl.ds(1, 1))
            send(velocity, v_raw, dv, dw, H - 1, pl.ds(0, 1))
            send(velocity, v_raw, dv, dw, H - 1, pl.ds(2, 1))
        else:
            send(velocity, v_raw, dv, dw, H - 1, pl.ds(0, 3))
        send(source, s_raw, dv, dw, H - 2 if dv and dw else H - 1)

    def send_tracer(dv, dw):
        block = c0.at[own_planes, own_rows]
        send(block, c0, dv, dw, H - 1 if dv and dw else H)

    levels = (c0, c1, c2, c3, c4)
    below_top = lax.broadcasted_iota(jnp.int32, (1, nz), 1) < nz - 1

    def prepare(first, count, windows, unroll, shift="load"):
        def body(p, here_cs):
            return tuple(cells(p, row, rows, here_c) for (row, rows), here_c in zip(windows, here_cs))

        def cells(p, row, rows, here_c):
            here = pl.ds(row, rows)
            next_c = c0[p + 1, here, :]
            up_c = pltpu.roll(here_c, rows - 1, 0) if shift == "roll" else c0[p, pl.ds(row + 1, rows), :]
            open_here = here_c > 0.0
            wx[p, here, :] = jnp.where(jnp.minimum(here_c, next_c) > 0.0, v_raw[0, p, here, :], 0.0)
            wy[p, here, :] = jnp.where(jnp.minimum(here_c, up_c) > 0.0, v_raw[1, p, here, :], 0.0)
            wz[p, here, :] = jnp.where(open_here & below_top, v_raw[2, p, here, :], 0.0)
            src[p, here, :] = jnp.where(open_here, s_raw[p, here, :], 0.0)
            return next_c

        sweep(first, count, unroll, body, tuple(c0[first, pl.ds(row, rows), :] for row, rows in windows))

    def advance(step, first, count, windows, unroll, shift="load", shade=None, carries=None):
        old, new = levels[step - 1], levels[step]

        def body(p, states):
            return tuple(cells(p, row, rows, state) for (row, rows), state in zip(windows, states))

        def cells(p, row, rows, state):
            here_c, flux_low, carry = state
            here, up, low = pl.ds(row, rows), pl.ds(row + 1, rows), pl.ds(row - 1, rows)
            next_c = old[p + 1, here, :]
            flux_x = flux(wx[p, here, :], here_c, next_c)
            wy_here = wy[p, here, :]
            if shift == "roll":
                flux_y = flux(wy_here, here_c, pltpu.roll(here_c, rows - 1, 0))
                flux_y_low = pltpu.roll(flux_y, 1, 0)
            else:
                flux_y = flux(wy_here, here_c, old[p, up, :])
                flux_y_low = flux(wy[p, low, :], old[p, low, :], here_c)
            flux_z = flux(wz[p, here, :], here_c, pltpu.roll(here_c, nz - 1, 1))
            flux_z_low = pltpu.roll(flux_z, 1, 1)
            value = here_c + src[p, here, :] - (flux_x - flux_low) - (flux_y - flux_y_low) - (flux_z - flux_z_low)
            new[p, here, :] = value
            if shade is not None:
                carry = shade(value, c0[p, here, :], carry)
            return next_c, flux_x, carry

        states = []
        for i, (row, rows) in enumerate(windows):
            here = pl.ds(row, rows)
            here_c = old[first, here, :]
            flux_low = flux(wx[first - 1, here, :], old[first - 1, here, :], here_c)
            states.append((here_c, flux_low, carries[i] if carries else ()))
        return tuple(state[2] for state in sweep(first, count, unroll, body, tuple(states)))

    scale = LOG2E / (nx * views)

    def shade(value, start, carry):
        depth, through, red, green, blue = carry
        wall = start <= 0.0
        depth = depth + jnp.where(wall, 4.0, value) * scale
        after = jnp.exp2(-depth)
        weight = through - after
        shading = value / (1.0 + value)
        red = red + weight * jnp.where(wall, 0.55, shading)
        green = green + weight * jnp.where(wall, 0.5, jnp.exp2(value * (-0.5 * LOG2E)))
        blue = blue + weight * jnp.where(wall, 0.45, 0.2 + 0.6 * (shading * shading))
        return depth, after, red, green, blue

    def nothing(rows):
        zero = jnp.zeros((rows, nz), jnp.float32)
        return zero, jnp.ones((rows, nz), jnp.float32), zero, zero, zero

    x0 = H + 1
    last = x0 + nx - 1
    own, middle = [(Y0, ny)], [(Y0 + H, ny - 2 * H)]
    for side in near:
        send_inputs(*side)
    tell(0, near)
    for load in loads[:2]:
        load.wait()

    def mask_plane(p, carry):
        c0[p, own_rows, :] = jnp.where(b_raw[p - x0] == 0, t_raw[p - x0], 0.0)
        return carry

    sweep(x0, nx, 16, mask_plane, 0)
    for side in near:
        send_tracer(*side)
    pl.semaphore_wait(known_sem.at[0], len(near))
    if views // 2 > 2:
        tell(1, near[:2])
    for side in corners:
        send_inputs(*side)
        send_tracer(*side)
    for load in loads[2:]:
        load.wait()
    prepare(x0, nx - 1, own, 8, "roll")
    for step in range(1, STEPS):
        advance(step, x0 + step, nx - 2 * step, own, 8, "roll")
        ring = step
        if ring < views // 2 - 1:
            pl.semaphore_wait(known_sem.at[ring], 2)
            if ring < views // 2 - 2:
                tell(ring + 1, near[:2])
    centre = advance(STEPS, x0 + H, nx - 2 * H, middle, 8, "load", shade, [nothing(ny - 2 * H)])[0]
    for i in range(5):
        mid_acc[i] = centre[i]

    for copy in sends:
        copy.wait_recv()
    edges = [(Y0 - H, 2 * H), (Y0 + ny - H, 2 * H)]
    prepare(1, nx + 2 * H, edges, 24)
    prepare(1, H, middle, H)
    prepare(last, H + 1, middle, H + 1)
    for step in range(1, STEPS):
        advance(step, x0 - H + step, nx + 2 * H - 2 * step, edges, 28)
        advance(step, x0 - H + step, H, middle, H)
        advance(step, x0 + nx - step, H, middle, H)
    left, right = advance(STEPS, x0, nx, edges, 16, "load", shade, [nothing(2 * H)] * 2)
    front = advance(STEPS, x0, H, middle, H, "load", shade, [nothing(ny - 2 * H)])[0]
    depth = front[0] + mid_acc[0]
    centre = (depth, jnp.exp2(-depth)) + tuple(front[i] + front[1] * mid_acc[i] for i in (2, 3, 4))
    centre = advance(STEPS, x0 + nx - H, H, middle, H, "load", shade, [centre])[0]
    for i in range(5):
        acc[i, 0:2 * H] = left[i]
        acc[i, 2 * H:ny] = centre[i]
        acc[i, ny:ny + 2 * H] = right[i]

    store = pltpu.make_async_copy(c4.at[own_planes, own_rows], out, out_sem)
    store.start()

    stacked = jnp.concatenate([acc[i, H:H + ny] for i in (2, 3, 4, 1)], axis=0)
    part[...] = stacked.T
    share = nz // views
    copies = []
    for hop in range(1, views):
        target = lax.rem(my_view + hop, views)
        copy = pltpu.make_async_remote_copy(
            src_ref=part.at[pl.ds(pl.multiple_of(target * share, share), share)],
            dst_ref=pieces.at[my_view],
            send_sem=piece_send.at[hop - 1], recv_sem=piece_recv.at[hop - 1],
            device_id=device(hop, 0), device_id_type=MESH,
        )
        copy.start()
        copies.append(copy)
    pieces[my_view] = part[pl.ds(pl.multiple_of(my_view * share, share), share), :]
    for copy in copies:
        copy.wait_recv()
    lane = lax.broadcasted_iota(jnp.int32, (share, 4 * ny), 1)
    colors = jnp.zeros((share, 4 * ny), jnp.float32)
    through = jnp.ones((share, 4 * ny), jnp.float32)
    for brick in range(views):
        piece = pieces[brick]
        spread = piece
        for group in range(3):
            turned = pltpu.roll(piece, (group + 1) * ny, 1)
            spread = jnp.where(lane // ny == group, turned, spread)
        colors = colors + through * piece
        through = through * spread
    pixels = jnp.where(lane < 3 * ny, colors, 1.0 - through)
    for i in range(4):
        picture[i] = pixels[:, i * ny:(i + 1) * ny]

    for copy in sends + copies:
        copy.wait_send()
    store.wait()


def on_device(tracer, velocity, buildings, source):
    nx, ny, nz = tracer.shape
    views, wides = lax.axis_size("view"), lax.axis_size("wide")
    field = (nx + 2 * H + 2, ny + 2 * Y0, nz)
    buffer = pltpu.VMEM(field, jnp.float32)
    n_sends = 40
    tracer_next, picture = pl.pallas_call(
        functools.partial(kernel, nx, ny, nz, views, wides),
        out_shape=(
            jax.ShapeDtypeStruct((nx, ny, nz), jnp.float32),
            jax.ShapeDtypeStruct((4, nz // views, ny), jnp.float32),
        ),
        in_specs=[pl.BlockSpec(memory_space=pltpu.HBM)] * 4,
        out_specs=(pl.BlockSpec(memory_space=pltpu.HBM), pl.BlockSpec(memory_space=pltpu.VMEM)),
        scratch_shapes=[
            pltpu.VMEM((nx, ny, nz), jnp.float32),
            pltpu.VMEM((3,) + field, jnp.float32),
            pltpu.VMEM((nx, ny, nz), jnp.int32),
        ]
        + [buffer] * 10
        + [
            pltpu.VMEM((5, ny + 2 * H, nz), jnp.float32),
            pltpu.VMEM((5, ny - 2 * H, nz), jnp.float32),
            pltpu.VMEM((nz, 4 * ny), jnp.float32),
            pltpu.VMEM((views, nz // views, 4 * ny), jnp.float32),
            pltpu.SemaphoreType.DMA((4,)),
            pltpu.SemaphoreType.DMA,
            pltpu.SemaphoreType.REGULAR((views // 2 - 1,)),
            pltpu.SemaphoreType.DMA((n_sends,)),
            pltpu.SemaphoreType.DMA((n_sends,)),
            pltpu.SemaphoreType.DMA((views - 1,)),
            pltpu.SemaphoreType.DMA((views - 1,)),
        ],
        compiler_params=pltpu.CompilerParams(
            collective_id=0, has_side_effects=True, vmem_limit_bytes=52 * 1024 * 1024
        ),
    )(tracer, velocity, buildings, source)
    return tracer_next, jnp.swapaxes(picture, 1, 2)


def solution(mesh):
    return jax.shard_map(
        on_device,
        mesh=mesh,
        in_specs=(
            P("view", "wide", None),
            P(None, "view", "wide", None),
            P("view", "wide", None),
            P("view", "wide", None),
        ),
        out_specs=(P("view", "wide", None), P(None, "wide", "view")),
        check_vma=False,
    )
```

```python
import functools
import math

import jax
import jax.numpy as jnp
from jax import lax
from jax.experimental import pallas as pl
from jax.experimental.pallas import tpu as pltpu
from jax.sharding import PartitionSpec as P

STEPS = 4
H = STEPS
Y0 = 8
MESH = pl.DeviceIdType.MESH
LOG2E = math.log2(math.e)


def sweep(start, count, unroll, body, carry):
    trips = count // unroll

    def chunk(trip, carry):
        first = start + trip * unroll
        for offset in range(unroll):
            carry = body(first + offset, carry)
        return carry

    if trips > 1:
        carry = lax.fori_loop(0, trips, chunk, carry)
    elif trips == 1:
        carry = chunk(0, carry)
    for offset in range(trips * unroll, count):
        carry = body(start + offset, carry)
    return carry


def flux(speed, lower, upper):
    return jnp.where(speed > 0.0, lower, upper) * speed


def face_range(side, size, depth):
    if side == 0:
        return 0, 0, size
    if side > 0:
        return size - depth, -depth, depth
    return 0, size, depth


def kernel(
    nx, ny, nz, views, wides, split,
    tracer, velocity, buildings, source,
    out, picture,
    t_raw, v_raw, b_raw, s_raw, wx, wy, wz, src, c0, c1, c2, c3, c4,
    acc, mid_acc, part, pieces,
    local_sem, out_sem, known_sem, send_sem, recv_sem, piece_send, piece_recv,
):
    my_view, my_wide = lax.axis_index("view"), lax.axis_index("wide")

    def device(dv, dw):
        return (lax.rem(my_view + dv + views, views), lax.rem(my_wide + dw + wides, wides))

    near = [(1, 0), (-1, 0), (0, 1), (0, -1)]
    corners = [(dv, dw) for dv in (1, -1) for dw in (1, -1)]

    own_planes, own_rows = pl.ds(H + 1, nx), pl.ds(Y0, ny)
    loads = [
        pltpu.make_async_copy(buildings, b_raw, local_sem.at[0]),
        pltpu.make_async_copy(tracer, t_raw, local_sem.at[1]),
        pltpu.make_async_copy(velocity, v_raw.at[:, own_planes, own_rows], local_sem.at[2]),
        pltpu.make_async_copy(source, s_raw.at[own_planes, own_rows], local_sem.at[3]),
    ]
    for load in loads:
        load.start()

    barrier = pltpu.get_barrier_semaphore()
    for dv, dw in near:
        pl.semaphore_signal(barrier, inc=1, device_id=device(dv, dw), device_id_type=MESH)
    pl.semaphore_wait(barrier, len(near))

    def tell(ring, sides):
        for dv, dw in sides:
            pl.semaphore_signal(known_sem.at[ring], inc=1, device_id=device(dv, dw), device_id_type=MESH)

    sends = []

    def send(ref, buffer, dv, dw, depth, pick=None, part=None):
        xs, xd, xn = face_range(dv, nx, depth)
        if part is not None:
            xs, xn = ((0, split), (split, nx - split))[part]
            xd = xs
        ys, yd, yn = face_range(dw, ny, depth)
        here = (pl.ds(xs, xn), pl.ds(ys, yn))
        there = (pl.ds(xd + H + 1, xn), pl.ds(yd + Y0, yn))
        if pick is not None:
            here, there = (pick,) + here, (pick,) + there
        index = len(sends)
        copy = pltpu.make_async_remote_copy(
            src_ref=ref.at[here], dst_ref=buffer.at[there],
            send_sem=send_sem.at[index], recv_sem=recv_sem.at[index],
            device_id=device(dv, dw), device_id_type=MESH,
        )
        copy.start()
        sends.append((copy, part))

    def send_inputs(dv, dw, part=None):
        if (dv, dw) == (1, 0):
            send(velocity, v_raw, dv, dw, H, pl.ds(0, 1), part)
            send(velocity, v_raw, dv, dw, H - 1, pl.ds(1, 2), part)
        elif (dv, dw) == (0, 1):
            send(velocity, v_raw, dv, dw, H, pl.ds(1, 1), part)
            send(velocity, v_raw, dv, dw, H - 1, pl.ds(0, 1), part)
            send(velocity, v_raw, dv, dw, H - 1, pl.ds(2, 1), part)
        else:
            send(velocity, v_raw, dv, dw, H - 1, pl.ds(0, 3), part)
        send(source, s_raw, dv, dw, H - 2 if dv and dw else H - 1, None, part)

    def send_tracer(dv, dw, part=None):
        block = c0.at[own_planes, own_rows]
        send(block, c0, dv, dw, H - 1 if dv and dw else H, None, part)

    levels = (c0, c1, c2, c3, c4)
    below_top = lax.broadcasted_iota(jnp.int32, (1, nz), 1) < nz - 1

    def prepare(first, count, windows, unroll, shift="load"):
        def body(p, here_cs):
            return tuple(cells(p, row, rows, here_c) for (row, rows), here_c in zip(windows, here_cs))

        def cells(p, row, rows, here_c):
            here = pl.ds(row, rows)
            next_c = c0[p + 1, here, :]
            up_c = pltpu.roll(here_c, rows - 1, 0) if shift == "roll" else c0[p, pl.ds(row + 1, rows), :]
            open_here = here_c > 0.0
            wx[p, here, :] = jnp.where(jnp.minimum(here_c, next_c) > 0.0, v_raw[0, p, here, :], 0.0)
            wy[p, here, :] = jnp.where(jnp.minimum(here_c, up_c) > 0.0, v_raw[1, p, here, :], 0.0)
            wz[p, here, :] = jnp.where(open_here & below_top, v_raw[2, p, here, :], 0.0)
            src[p, here, :] = jnp.where(open_here, s_raw[p, here, :], 0.0)
            return next_c

        sweep(first, count, unroll, body, tuple(c0[first, pl.ds(row, rows), :] for row, rows in windows))

    def advance(step, first, count, windows, unroll, shift="load", shade=None, carries=None):
        old, new = levels[step - 1], levels[step]

        def body(p, states):
            return tuple(cells(p, row, rows, state) for (row, rows), state in zip(windows, states))

        def cells(p, row, rows, state):
            here_c, flux_low, carry = state
            here, up, low = pl.ds(row, rows), pl.ds(row + 1, rows), pl.ds(row - 1, rows)
            next_c = old[p + 1, here, :]
            flux_x = flux(wx[p, here, :], here_c, next_c)
            wy_here = wy[p, here, :]
            if shift == "roll":
                flux_y = flux(wy_here, here_c, pltpu.roll(here_c, rows - 1, 0))
                flux_y_low = pltpu.roll(flux_y, 1, 0)
            else:
                flux_y = flux(wy_here, here_c, old[p, up, :])
                flux_y_low = flux(wy[p, low, :], old[p, low, :], here_c)
            flux_z = flux(wz[p, here, :], here_c, pltpu.roll(here_c, nz - 1, 1))
            flux_z_low = pltpu.roll(flux_z, 1, 1)
            value = here_c + src[p, here, :] - (flux_x - flux_low) - (flux_y - flux_y_low) - (flux_z - flux_z_low)
            new[p, here, :] = value
            if shade is not None:
                carry = shade(value, c0[p, here, :], carry)
            return next_c, flux_x, carry

        states = []
        for i, (row, rows) in enumerate(windows):
            here = pl.ds(row, rows)
            here_c = old[first, here, :]
            flux_low = flux(wx[first - 1, here, :], old[first - 1, here, :], here_c)
            states.append((here_c, flux_low, carries[i] if carries else ()))
        return tuple(state[2] for state in sweep(first, count, unroll, body, tuple(states)))

    scale = LOG2E / (nx * views)

    def shade(value, start, carry):
        depth, through, red, green, blue = carry
        wall = start <= 0.0
        depth = depth + jnp.where(wall, 4.0, value) * scale
        after = jnp.exp2(-depth)
        weight = through - after
        shading = value / (1.0 + value)
        red = red + weight * jnp.where(wall, 0.55, shading)
        green = green + weight * jnp.where(wall, 0.5, jnp.exp2(value * (-0.5 * LOG2E)))
        blue = blue + weight * jnp.where(wall, 0.45, 0.2 + 0.6 * (shading * shading))
        return depth, after, red, green, blue

    def behind(front, back):
        depth = front[0] + back[0]
        return (depth, jnp.exp2(-depth)) + tuple(front[i] + front[1] * back[i] for i in (2, 3, 4))

    def nothing(rows):
        zero = jnp.zeros((rows, nz), jnp.float32)
        return zero, jnp.ones((rows, nz), jnp.float32), zero, zero, zero

    x0 = H + 1
    last = x0 + nx - 1
    own, middle, wide = [(Y0, ny)], [(Y0 + H, ny - 2 * H)], [(Y0 - H, ny + 2 * H)]
    along, across = near[:2], near[2:]
    for side in across:
        send_inputs(*side, 0)
    for side in along:
        send_inputs(*side)
    tell(0, near)
    for load in loads[:2]:
        load.wait()

    def mask_plane(p, carry):
        c0[p, own_rows, :] = jnp.where(b_raw[p - x0] == 0, t_raw[p - x0], 0.0)
        return carry

    sweep(x0, nx, 16, mask_plane, 0)
    for side in across:
        send_tracer(*side, 0)
    early = [copy for copy, half in sends if half == 0]
    for side in along:
        send_tracer(*side)
    for side in across:
        send_inputs(*side, 1)
        send_tracer(*side, 1)
    pl.semaphore_wait(known_sem.at[0], len(near))
    if views // 2 > 2:
        tell(1, near[:2])
    for side in corners:
        send_inputs(*side)
        send_tracer(*side)
    for load in loads[2:]:
        load.wait()
    prepare(x0, nx - 1, own, 8, "roll")
    for step in range(1, STEPS):
        advance(step, x0 + step, nx - 2 * step, own, 8, "roll")
        ring = step
        if ring < views // 2 - 1:
            pl.semaphore_wait(known_sem.at[ring], 2)
            if ring < views // 2 - 2:
                tell(ring + 1, near[:2])
    centre = advance(STEPS, x0 + H, nx - 2 * H, middle, 8, "load", shade, [nothing(ny - 2 * H)])[0]
    for i in range(5):
        mid_acc[i] = centre[i]

    for copy in early:
        copy.wait_recv()
    edges = [(Y0 - H, 2 * H), (Y0 + ny - H, 2 * H)]
    prepare(x0, split - 1, edges, 20)
    for step in range(1, STEPS):
        advance(step, x0 + step, split - 2 * step, edges, 20)
    early_edges = advance(STEPS, x0 + H, split - 2 * H, edges, 16, "load", shade, [nothing(2 * H)] * 2)
    for copy, half in sends:
        if half != 0:
            copy.wait_recv()
    prepare(1, H, wide, H)
    prepare(x0 + split - 1, nx - split + H + 1, edges, 28)
    prepare(last, H + 1, middle, H + 1)
    for step in range(1, STEPS):
        advance(step, x0 - H + step, H, wide, H)
        advance(step, x0 + split - step, nx - split + H, edges, 28)
        advance(step, x0 + nx - step, H, middle, H)
    front_edges = advance(STEPS, x0, H, edges, H, "load", shade, [nothing(2 * H)] * 2)
    edge_carries = [behind(f, b) for f, b in zip(front_edges, early_edges)]
    left, right = advance(STEPS, x0 + split - H, nx - split + H, edges, 18, "load", shade, edge_carries)
    front = advance(STEPS, x0, H, middle, H, "load", shade, [nothing(ny - 2 * H)])[0]
    centre = behind(front, [mid_acc[i] for i in range(5)])
    centre = advance(STEPS, x0 + nx - H, H, middle, H, "load", shade, [centre])[0]
    for i in range(5):
        acc[i, 0:2 * H] = left[i]
        acc[i, 2 * H:ny] = centre[i]
        acc[i, ny:ny + 2 * H] = right[i]

    store = pltpu.make_async_copy(c4.at[own_planes, own_rows], out, out_sem)
    store.start()

    stacked = jnp.concatenate([acc[i, H:H + ny] for i in (2, 3, 4, 1)], axis=0)
    part[...] = stacked.T
    share = nz // views
    copies = []
    for hop in sorted(range(1, views), key=lambda hop: -min(hop, views - hop)):
        target = lax.rem(my_view + hop, views)
        copy = pltpu.make_async_remote_copy(
            src_ref=part.at[pl.ds(pl.multiple_of(target * share, share), share)],
            dst_ref=pieces.at[my_view],
            send_sem=piece_send.at[hop - 1], recv_sem=piece_recv.at[hop - 1],
            device_id=device(hop, 0), device_id_type=MESH,
        )
        copy.start()
        copies.append(copy)
    pieces[my_view] = part[pl.ds(pl.multiple_of(my_view * share, share), share), :]
    for copy in copies:
        copy.wait_recv()
    lane = lax.broadcasted_iota(jnp.int32, (share, 4 * ny), 1)
    colors = jnp.zeros((share, 4 * ny), jnp.float32)
    through = jnp.ones((share, 4 * ny), jnp.float32)
    for brick in range(views):
        piece = pieces[brick]
        spread = piece
        for group in range(3):
            turned = pltpu.roll(piece, (group + 1) * ny, 1)
            spread = jnp.where(lane // ny == group, turned, spread)
        colors = colors + through * piece
        through = through * spread
    pixels = jnp.where(lane < 3 * ny, colors, 1.0 - through)
    for i in range(4):
        picture[i] = pixels[:, i * ny:(i + 1) * ny]

    for copy in [copy for copy, half in sends] + copies:
        copy.wait_send()
    store.wait()


def finish(tracer_next, picture, tracer_out, picture_out, sem):
    planes = tracer_next.shape[0]
    parts = 8
    each = planes // parts
    copies = [pltpu.make_async_copy(picture, picture_out, sem.at[parts])]
    for i in range(parts):
        here = pl.ds(i * each, each)
        copies.append(pltpu.make_async_copy(tracer_next.at[here], tracer_out.at[here], sem.at[i]))
    for copy in copies:
        copy.start()
    for copy in copies:
        copy.wait()


def on_device(tracer, velocity, buildings, source):
    nx, ny, nz = tracer.shape
    views, wides = lax.axis_size("view"), lax.axis_size("wide")
    field = (nx + 2 * H + 2, ny + 2 * Y0, nz)
    buffer = pltpu.VMEM(field, jnp.float32)
    n_sends = 40
    tracer_next, picture = pl.pallas_call(
        functools.partial(kernel, nx, ny, nz, views, wides, nx * 5 // 8),
        out_shape=(
            jax.ShapeDtypeStruct((nx, ny, nz), jnp.float32),
            jax.ShapeDtypeStruct((4, nz // views, ny), jnp.float32),
        ),
        in_specs=[pl.BlockSpec(memory_space=pltpu.HBM)] * 4,
        out_specs=(pl.BlockSpec(memory_space=pltpu.HBM), pl.BlockSpec(memory_space=pltpu.VMEM)),
        scratch_shapes=[
            pltpu.VMEM((nx, ny, nz), jnp.float32),
            pltpu.VMEM((3,) + field, jnp.float32),
            pltpu.VMEM((nx, ny, nz), jnp.int32),
        ]
        + [buffer] * 10
        + [
            pltpu.VMEM((5, ny + 2 * H, nz), jnp.float32),
            pltpu.VMEM((5, ny - 2 * H, nz), jnp.float32),
            pltpu.VMEM((nz, 4 * ny), jnp.float32),
            pltpu.VMEM((views, nz // views, 4 * ny), jnp.float32),
            pltpu.SemaphoreType.DMA((4,)),
            pltpu.SemaphoreType.DMA,
            pltpu.SemaphoreType.REGULAR((views // 2 - 1,)),
            pltpu.SemaphoreType.DMA((n_sends,)),
            pltpu.SemaphoreType.DMA((n_sends,)),
            pltpu.SemaphoreType.DMA((views - 1,)),
            pltpu.SemaphoreType.DMA((views - 1,)),
        ],
        compiler_params=pltpu.CompilerParams(
            collective_id=0, has_side_effects=True, vmem_limit_bytes=52 * 1024 * 1024
        ),
    )(tracer, velocity, buildings, source)
    tracer_next, picture = pl.pallas_call(
        finish,
        out_shape=(
            jax.ShapeDtypeStruct(tracer_next.shape, jnp.float32),
            jax.ShapeDtypeStruct(picture.shape, jnp.float32),
        ),
        in_specs=[pl.BlockSpec(memory_space=pl.ANY)] * 2,
        out_specs=(pl.BlockSpec(memory_space=pltpu.HBM),) * 2,
        scratch_shapes=[pltpu.SemaphoreType.DMA((9,))],
        compiler_params=pltpu.CompilerParams(vmem_limit_bytes=1024 * 1024),
    )(tracer_next, picture)
    return tracer_next, jnp.swapaxes(picture, 1, 2)


def solution(mesh):
    return jax.shard_map(
        on_device,
        mesh=mesh,
        in_specs=(
            P("view", "wide", None),
            P(None, "view", "wide", None),
            P("view", "wide", None),
            P("view", "wide", None),
        ),
        out_specs=(P("view", "wide", None), P(None, "wide", "view")),
        check_vma=False,
    )
```

```python
import functools
import math

import jax
import jax.numpy as jnp
from jax import lax
from jax.experimental import pallas as pl
from jax.experimental.pallas import tpu as pltpu
from jax.sharding import PartitionSpec as P

STEPS = 4
H = STEPS
Y0 = 8
MESH = pl.DeviceIdType.MESH
LOG2E = math.log2(math.e)


def sweep(start, count, unroll, body, carry):
    trips = count // unroll

    def chunk(trip, carry):
        first = start + trip * unroll
        for offset in range(unroll):
            carry = body(first + offset, carry)
        return carry

    if trips > 1:
        carry = lax.fori_loop(0, trips, chunk, carry)
    elif trips == 1:
        carry = chunk(0, carry)
    for offset in range(trips * unroll, count):
        carry = body(start + offset, carry)
    return carry


def flux(speed, lower, upper):
    return jnp.where(speed > 0.0, lower, upper) * speed


def face_range(side, size, depth):
    if side == 0:
        return 0, 0, size
    if side > 0:
        return size - depth, -depth, depth
    return 0, size, depth


def kernel(
    nx, ny, nz, views, wides, split,
    tracer, velocity, buildings, source,
    out, picture,
    t_raw, v_raw, b_raw, s_raw, wx, wy, wz, src, c0, c1, c2, c3, c4,
    acc, mid_acc, part, pieces,
    local_sem, out_sem, known_sem, send_sem, recv_sem, piece_send, piece_recv,
):
    my_view, my_wide = lax.axis_index("view"), lax.axis_index("wide")

    def device(dv, dw):
        return (lax.rem(my_view + dv + views, views), lax.rem(my_wide + dw + wides, wides))

    near = [(1, 0), (-1, 0), (0, 1), (0, -1)]
    corners = [(dv, dw) for dv in (1, -1) for dw in (1, -1)]

    own_planes, own_rows = pl.ds(H + 1, nx), pl.ds(Y0, ny)
    loads = [
        pltpu.make_async_copy(buildings, b_raw, local_sem.at[0]),
        pltpu.make_async_copy(tracer, t_raw, local_sem.at[1]),
        pltpu.make_async_copy(velocity, v_raw.at[:, own_planes, own_rows], local_sem.at[2]),
        pltpu.make_async_copy(source, s_raw.at[own_planes, own_rows], local_sem.at[3]),
    ]
    for load in loads:
        load.start()

    barrier = pltpu.get_barrier_semaphore()
    for dv, dw in near:
        pl.semaphore_signal(barrier, inc=1, device_id=device(dv, dw), device_id_type=MESH)
    pl.semaphore_wait(barrier, len(near))

    def tell(ring, sides):
        for dv, dw in sides:
            pl.semaphore_signal(known_sem.at[ring], inc=1, device_id=device(dv, dw), device_id_type=MESH)

    sends = []

    def send(ref, buffer, dv, dw, depth, pick=None, part=None):
        xs, xd, xn = face_range(dv, nx, depth)
        if part is not None:
            xs, xn = ((0, split), (split, nx - split))[part]
            xd = xs
        ys, yd, yn = face_range(dw, ny, depth)
        here = (pl.ds(xs, xn), pl.ds(ys, yn))
        there = (pl.ds(xd + H + 1, xn), pl.ds(yd + Y0, yn))
        if pick is not None:
            here, there = (pick,) + here, (pick,) + there
        index = len(sends)
        copy = pltpu.make_async_remote_copy(
            src_ref=ref.at[here], dst_ref=buffer.at[there],
            send_sem=send_sem.at[index], recv_sem=recv_sem.at[index],
            device_id=device(dv, dw), device_id_type=MESH,
        )
        copy.start()
        sends.append((copy, part))

    def send_inputs(dv, dw, part=None):
        if (dv, dw) == (1, 0):
            send(velocity, v_raw, dv, dw, H, pl.ds(0, 1), part)
            send(velocity, v_raw, dv, dw, H - 1, pl.ds(1, 2), part)
        elif (dv, dw) == (0, 1):
            send(velocity, v_raw, dv, dw, H, pl.ds(1, 1), part)
            send(velocity, v_raw, dv, dw, H - 1, pl.ds(0, 1), part)
            send(velocity, v_raw, dv, dw, H - 1, pl.ds(2, 1), part)
        else:
            send(velocity, v_raw, dv, dw, H - 1, pl.ds(0, 3), part)
        send(source, s_raw, dv, dw, H - 2 if dv and dw else H - 1, None, part)

    def send_tracer(dv, dw, part=None):
        block = c0.at[own_planes, own_rows]
        send(block, c0, dv, dw, H - 1 if dv and dw else H, None, part)

    levels = (c0, c1, c2, c3, c4)
    below_top = lax.broadcasted_iota(jnp.int32, (1, nz), 1) < nz - 1

    def prepare(first, count, windows, unroll, shift="load"):
        def body(p, here_cs):
            return tuple(cells(p, row, rows, here_c) for (row, rows), here_c in zip(windows, here_cs))

        def cells(p, row, rows, here_c):
            here = pl.ds(row, rows)
            next_c = c0[p + 1, here, :]
            up_c = pltpu.roll(here_c, rows - 1, 0) if shift == "roll" else c0[p, pl.ds(row + 1, rows), :]
            open_here = here_c > 0.0
            wx[p, here, :] = jnp.where(jnp.minimum(here_c, next_c) > 0.0, v_raw[0, p, here, :], 0.0)
            wy[p, here, :] = jnp.where(jnp.minimum(here_c, up_c) > 0.0, v_raw[1, p, here, :], 0.0)
            wz[p, here, :] = jnp.where(open_here & below_top, v_raw[2, p, here, :], 0.0)
            src[p, here, :] = jnp.where(open_here, s_raw[p, here, :], 0.0)
            return next_c

        sweep(first, count, unroll, body, tuple(c0[first, pl.ds(row, rows), :] for row, rows in windows))

    def advance(step, first, count, windows, unroll, shift="load", shade=None, carries=None):
        old, new = levels[step - 1], levels[step]

        def body(p, states):
            return tuple(cells(p, row, rows, state) for (row, rows), state in zip(windows, states))

        def cells(p, row, rows, state):
            here_c, flux_low, carry = state
            here, up, low = pl.ds(row, rows), pl.ds(row + 1, rows), pl.ds(row - 1, rows)
            next_c = old[p + 1, here, :]
            flux_x = flux(wx[p, here, :], here_c, next_c)
            wy_here = wy[p, here, :]
            if shift == "roll":
                flux_y = flux(wy_here, here_c, pltpu.roll(here_c, rows - 1, 0))
                flux_y_low = pltpu.roll(flux_y, 1, 0)
            else:
                flux_y = flux(wy_here, here_c, old[p, up, :])
                flux_y_low = flux(wy[p, low, :], old[p, low, :], here_c)
            flux_z = flux(wz[p, here, :], here_c, pltpu.roll(here_c, nz - 1, 1))
            flux_z_low = pltpu.roll(flux_z, 1, 1)
            value = here_c + src[p, here, :] - (flux_x - flux_low) - (flux_y - flux_y_low) - (flux_z - flux_z_low)
            new[p, here, :] = value
            if shade is not None:
                carry = shade(value, c0[p, here, :], carry)
            return next_c, flux_x, carry

        states = []
        for i, (row, rows) in enumerate(windows):
            here = pl.ds(row, rows)
            here_c = old[first, here, :]
            flux_low = flux(wx[first - 1, here, :], old[first - 1, here, :], here_c)
            states.append((here_c, flux_low, carries[i] if carries else ()))
        return tuple(state[2] for state in sweep(first, count, unroll, body, tuple(states)))

    scale = LOG2E / (nx * views)

    def shade(value, start, carry):
        depth, through, red, green, blue = carry
        wall = start <= 0.0
        depth = depth + jnp.where(wall, 4.0, value) * scale
        after = jnp.exp2(-depth)
        weight = through - after
        shading = value / (1.0 + value)
        red = red + weight * jnp.where(wall, 0.55, shading)
        green = green + weight * jnp.where(wall, 0.5, jnp.exp2(value * (-0.5 * LOG2E)))
        blue = blue + weight * jnp.where(wall, 0.45, 0.2 + 0.6 * (shading * shading))
        return depth, after, red, green, blue

    def behind(front, back):
        depth = front[0] + back[0]
        return (depth, jnp.exp2(-depth)) + tuple(front[i] + front[1] * back[i] for i in (2, 3, 4))

    def nothing(rows):
        zero = jnp.zeros((rows, nz), jnp.float32)
        return zero, jnp.ones((rows, nz), jnp.float32), zero, zero, zero

    x0 = H + 1
    last = x0 + nx - 1
    own, middle, wide = [(Y0, ny)], [(Y0 + H, ny - 2 * H)], [(Y0 - H, ny + 2 * H)]
    along, across = near[:2], near[2:]
    for side in across:
        send_inputs(*side, 0)
    for side in along:
        send_inputs(*side)
    tell(0, near)
    for load in loads[:2]:
        load.wait()

    def mask_plane(p, carry):
        c0[p, own_rows, :] = jnp.where(b_raw[p - x0] == 0, t_raw[p - x0], 0.0)
        return carry

    sweep(x0, nx, 16, mask_plane, 0)
    for side in across:
        send_tracer(*side, 0)
    early = [copy for copy, half in sends if half == 0]
    for side in along:
        send_tracer(*side)
    for side in across:
        send_inputs(*side, 1)
        send_tracer(*side, 1)
    pl.semaphore_wait(known_sem.at[0], len(near))
    if views // 2 > 2:
        tell(1, near[:2])
    for side in corners:
        send_inputs(*side)
        send_tracer(*side)
    for load in loads[2:]:
        load.wait()
    prepare(x0, nx - 1, own, 16, "roll")
    for step in range(1, STEPS):
        advance(step, x0 + step, nx - 2 * step, own, 16, "roll")
        ring = step
        if ring < views // 2 - 1:
            pl.semaphore_wait(known_sem.at[ring], 2)
            if ring < views // 2 - 2:
                tell(ring + 1, near[:2])
    centre = advance(STEPS, x0 + H, nx - 2 * H, middle, 8, "load", shade, [nothing(ny - 2 * H)])[0]
    for i in range(5):
        mid_acc[i] = centre[i]

    for copy in early:
        copy.wait_recv()
    edges = [(Y0 - H, 2 * H), (Y0 + ny - H, 2 * H)]
    prepare(x0, split - 1, edges, 20)
    for step in range(1, STEPS):
        advance(step, x0 + step, split - 2 * step, edges, 20)
    early_edges = advance(STEPS, x0 + H, split - 2 * H, edges, 16, "load", shade, [nothing(2 * H)] * 2)
    for copy, half in sends:
        if half != 0:
            copy.wait_recv()
    prepare(1, H, wide, H)
    prepare(x0 + split - 1, nx - split + H + 1, edges, 28)
    prepare(last, H + 1, middle, H + 1)
    for step in range(1, STEPS):
        advance(step, x0 - H + step, H, wide, H)
        advance(step, x0 + split - step, nx - split + H, edges, 28)
        advance(step, x0 + nx - step, H, middle, H)
    front_edges = advance(STEPS, x0, H, edges, H, "load", shade, [nothing(2 * H)] * 2)
    edge_carries = [behind(f, b) for f, b in zip(front_edges, early_edges)]
    left, right = advance(STEPS, x0 + split - H, nx - split + H, edges, 18, "load", shade, edge_carries)
    front = advance(STEPS, x0, H, middle, H, "load", shade, [nothing(ny - 2 * H)])[0]
    centre = behind(front, [mid_acc[i] for i in range(5)])
    centre = advance(STEPS, x0 + nx - H, H, middle, H, "load", shade, [centre])[0]
    for i in range(5):
        acc[i, 0:2 * H] = left[i]
        acc[i, 2 * H:ny] = centre[i]
        acc[i, ny:ny + 2 * H] = right[i]

    store = pltpu.make_async_copy(c4.at[own_planes, own_rows], out, out_sem)
    store.start()

    stacked = jnp.concatenate([acc[i, H:H + ny] for i in (2, 3, 4, 1)], axis=0)
    part[...] = stacked.T
    share = nz // views
    copies = []
    for hop in sorted(range(1, views), key=lambda hop: -min(hop, views - hop)):
        target = lax.rem(my_view + hop, views)
        copy = pltpu.make_async_remote_copy(
            src_ref=part.at[pl.ds(pl.multiple_of(target * share, share), share)],
            dst_ref=pieces.at[my_view],
            send_sem=piece_send.at[hop - 1], recv_sem=piece_recv.at[hop - 1],
            device_id=device(hop, 0), device_id_type=MESH,
        )
        copy.start()
        copies.append(copy)
    pieces[my_view] = part[pl.ds(pl.multiple_of(my_view * share, share), share), :]
    for copy in copies:
        copy.wait_recv()
    lane = lax.broadcasted_iota(jnp.int32, (share, 4 * ny), 1)
    colors = jnp.zeros((share, 4 * ny), jnp.float32)
    through = jnp.ones((share, 4 * ny), jnp.float32)
    for brick in range(views):
        piece = pieces[brick]
        spread = piece
        for group in range(3):
            turned = pltpu.roll(piece, (group + 1) * ny, 1)
            spread = jnp.where(lane // ny == group, turned, spread)
        colors = colors + through * piece
        through = through * spread
    pixels = jnp.where(lane < 3 * ny, colors, 1.0 - through)
    for i in range(4):
        picture[i] = pixels[:, i * ny:(i + 1) * ny]

    for copy in [copy for copy, half in sends] + copies:
        copy.wait_send()
    store.wait()


def finish(tracer_next, picture, tracer_out, picture_out, sem):
    planes = tracer_next.shape[0]
    parts = 8
    each = planes // parts
    copies = [pltpu.make_async_copy(picture, picture_out, sem.at[parts])]
    for i in range(parts):
        here = pl.ds(i * each, each)
        copies.append(pltpu.make_async_copy(tracer_next.at[here], tracer_out.at[here], sem.at[i]))
    for copy in copies:
        copy.start()
    for copy in copies:
        copy.wait()


def on_device(tracer, velocity, buildings, source):
    nx, ny, nz = tracer.shape
    views, wides = lax.axis_size("view"), lax.axis_size("wide")
    field = (nx + 2 * H + 2, ny + 2 * Y0, nz)
    buffer = pltpu.VMEM(field, jnp.float32)
    n_sends = 40
    tracer_next, picture = pl.pallas_call(
        functools.partial(kernel, nx, ny, nz, views, wides, nx * 5 // 8),
        out_shape=(
            jax.ShapeDtypeStruct((nx, ny, nz), jnp.float32),
            jax.ShapeDtypeStruct((4, nz // views, ny), jnp.float32),
        ),
        in_specs=[pl.BlockSpec(memory_space=pltpu.HBM)] * 4,
        out_specs=(pl.BlockSpec(memory_space=pltpu.HBM), pl.BlockSpec(memory_space=pltpu.VMEM)),
        scratch_shapes=[
            pltpu.VMEM((nx, ny, nz), jnp.float32),
            pltpu.VMEM((3,) + field, jnp.float32),
            pltpu.VMEM((nx, ny, nz), jnp.int32),
        ]
        + [buffer] * 10
        + [
            pltpu.VMEM((5, ny + 2 * H, nz), jnp.float32),
            pltpu.VMEM((5, ny - 2 * H, nz), jnp.float32),
            pltpu.VMEM((nz, 4 * ny), jnp.float32),
            pltpu.VMEM((views, nz // views, 4 * ny), jnp.float32),
            pltpu.SemaphoreType.DMA((4,)),
            pltpu.SemaphoreType.DMA,
            pltpu.SemaphoreType.REGULAR((views // 2 - 1,)),
            pltpu.SemaphoreType.DMA((n_sends,)),
            pltpu.SemaphoreType.DMA((n_sends,)),
            pltpu.SemaphoreType.DMA((views - 1,)),
            pltpu.SemaphoreType.DMA((views - 1,)),
        ],
        compiler_params=pltpu.CompilerParams(
            collective_id=0, has_side_effects=True, vmem_limit_bytes=52 * 1024 * 1024
        ),
    )(tracer, velocity, buildings, source)
    tracer_next, picture = pl.pallas_call(
        finish,
        out_shape=(
            jax.ShapeDtypeStruct(tracer_next.shape, jnp.float32),
            jax.ShapeDtypeStruct(picture.shape, jnp.float32),
        ),
        in_specs=[pl.BlockSpec(memory_space=pl.ANY)] * 2,
        out_specs=(pl.BlockSpec(memory_space=pltpu.HBM),) * 2,
        scratch_shapes=[pltpu.SemaphoreType.DMA((9,))],
        compiler_params=pltpu.CompilerParams(vmem_limit_bytes=1024 * 1024),
    )(tracer_next, picture)
    return tracer_next, jnp.swapaxes(picture, 1, 2)


def solution(mesh):
    return jax.shard_map(
        on_device,
        mesh=mesh,
        in_specs=(
            P("view", "wide", None),
            P(None, "view", "wide", None),
            P("view", "wide", None),
            P("view", "wide", None),
        ),
        out_specs=(P("view", "wide", None), P(None, "wide", "view")),
        check_vma=False,
    )
```

```python
import functools
import math

import jax
import jax.numpy as jnp
from jax import lax
from jax.experimental import pallas as pl
from jax.experimental.pallas import tpu as pltpu
from jax.sharding import PartitionSpec as P

STEPS = 4
H = STEPS
Y0 = 8
MESH = pl.DeviceIdType.MESH
LOG2E = math.log2(math.e)


def sweep(start, count, unroll, body, carry):
    trips = count // unroll

    def chunk(trip, carry):
        first = start + trip * unroll
        for offset in range(unroll):
            carry = body(first + offset, carry)
        return carry

    if trips > 1:
        carry = lax.fori_loop(0, trips, chunk, carry)
    elif trips == 1:
        carry = chunk(0, carry)
    for offset in range(trips * unroll, count):
        carry = body(start + offset, carry)
    return carry


def flux(speed, lower, upper):
    return jnp.where(speed > 0.0, lower, upper) * speed


def face_range(side, size, depth):
    if side == 0:
        return 0, 0, size
    if side > 0:
        return size - depth, -depth, depth
    return 0, size, depth


def kernel(
    nx, ny, nz, views, wides, split,
    tracer, velocity, buildings, source,
    out, picture,
    t_raw, v_raw, b_raw, s_raw, wx, wy, wz, src, c0, c1, c2, c3, c4,
    acc, mid_acc, part, pieces,
    local_sem, out_sem, known_sem, send_sem, recv_sem, piece_send, piece_recv,
):
    my_view, my_wide = lax.axis_index("view"), lax.axis_index("wide")

    def device(dv, dw):
        return (lax.rem(my_view + dv + views, views), lax.rem(my_wide + dw + wides, wides))

    near = [(1, 0), (-1, 0), (0, 1), (0, -1)]
    corners = [(dv, dw) for dv in (1, -1) for dw in (1, -1)]

    own_planes, own_rows = pl.ds(H + 1, nx), pl.ds(Y0, ny)
    loads = [
        pltpu.make_async_copy(buildings, b_raw, local_sem.at[0]),
        pltpu.make_async_copy(tracer, t_raw, local_sem.at[1]),
        pltpu.make_async_copy(velocity, v_raw.at[:, own_planes, own_rows], local_sem.at[2]),
        pltpu.make_async_copy(source, s_raw.at[own_planes, own_rows], local_sem.at[3]),
    ]
    for load in loads:
        load.start()

    barrier = pltpu.get_barrier_semaphore()
    for dv, dw in near:
        pl.semaphore_signal(barrier, inc=1, device_id=device(dv, dw), device_id_type=MESH)
    pl.semaphore_wait(barrier, len(near))

    def tell(ring, sides):
        for dv, dw in sides:
            pl.semaphore_signal(known_sem.at[ring], inc=1, device_id=device(dv, dw), device_id_type=MESH)

    sends = []

    def send(ref, buffer, dv, dw, depth, pick=None, part=None):
        xs, xd, xn = face_range(dv, nx, depth)
        if part is not None:
            xs, xn = ((0, split), (split, nx - split))[part]
            xd = xs
        ys, yd, yn = face_range(dw, ny, depth)
        here = (pl.ds(xs, xn), pl.ds(ys, yn))
        there = (pl.ds(xd + H + 1, xn), pl.ds(yd + Y0, yn))
        if pick is not None:
            here, there = (pick,) + here, (pick,) + there
        index = len(sends)
        copy = pltpu.make_async_remote_copy(
            src_ref=ref.at[here], dst_ref=buffer.at[there],
            send_sem=send_sem.at[index], recv_sem=recv_sem.at[index],
            device_id=device(dv, dw), device_id_type=MESH,
        )
        copy.start()
        sends.append((copy, part))

    def send_inputs(dv, dw, part=None):
        if (dv, dw) == (1, 0):
            send(velocity, v_raw, dv, dw, H, pl.ds(0, 1), part)
            send(velocity, v_raw, dv, dw, H - 1, pl.ds(1, 2), part)
        elif (dv, dw) == (0, 1):
            send(velocity, v_raw, dv, dw, H, pl.ds(1, 1), part)
            send(velocity, v_raw, dv, dw, H - 1, pl.ds(0, 1), part)
            send(velocity, v_raw, dv, dw, H - 1, pl.ds(2, 1), part)
        else:
            send(velocity, v_raw, dv, dw, H - 1, pl.ds(0, 3), part)
        send(source, s_raw, dv, dw, H - 2 if dv and dw else H - 1, None, part)

    def send_tracer(dv, dw, part=None):
        block = c0.at[own_planes, own_rows]
        send(block, c0, dv, dw, H - 1 if dv and dw else H, None, part)

    levels = (c0, c1, c2, c3, c4)
    below_top = lax.broadcasted_iota(jnp.int32, (1, nz), 1) < nz - 1

    def prepare(first, count, windows, unroll, shift="load"):
        def body(p, here_cs):
            return tuple(cells(p, row, rows, here_c) for (row, rows), here_c in zip(windows, here_cs))

        def cells(p, row, rows, here_c):
            here = pl.ds(row, rows)
            next_c = c0[p + 1, here, :]
            up_c = pltpu.roll(here_c, rows - 1, 0) if shift == "roll" else c0[p, pl.ds(row + 1, rows), :]
            open_here = here_c > 0.0
            wx[p, here, :] = jnp.where(jnp.minimum(here_c, next_c) > 0.0, v_raw[0, p, here, :], 0.0)
            wy[p, here, :] = jnp.where(jnp.minimum(here_c, up_c) > 0.0, v_raw[1, p, here, :], 0.0)
            wz[p, here, :] = jnp.where(open_here & below_top, v_raw[2, p, here, :], 0.0)
            src[p, here, :] = jnp.where(open_here, s_raw[p, here, :], 0.0)
            return next_c

        sweep(first, count, unroll, body, tuple(c0[first, pl.ds(row, rows), :] for row, rows in windows))

    def advance(step, first, count, windows, unroll, shift="load", shade=None, carries=None):
        old, new = levels[step - 1], levels[step]

        def body(p, states):
            return tuple(cells(p, row, rows, state) for (row, rows), state in zip(windows, states))

        def cells(p, row, rows, state):
            here_c, flux_low, carry = state
            here, up, low = pl.ds(row, rows), pl.ds(row + 1, rows), pl.ds(row - 1, rows)
            next_c = old[p + 1, here, :]
            flux_x = flux(wx[p, here, :], here_c, next_c)
            wy_here = wy[p, here, :]
            if shift == "roll":
                flux_y = flux(wy_here, here_c, pltpu.roll(here_c, rows - 1, 0))
                flux_y_low = pltpu.roll(flux_y, 1, 0)
            else:
                flux_y = flux(wy_here, here_c, old[p, up, :])
                flux_y_low = flux(wy[p, low, :], old[p, low, :], here_c)
            flux_z = flux(wz[p, here, :], here_c, pltpu.roll(here_c, nz - 1, 1))
            flux_z_low = pltpu.roll(flux_z, 1, 1)
            value = here_c + src[p, here, :] - (flux_x - flux_low) - (flux_y - flux_y_low) - (flux_z - flux_z_low)
            new[p, here, :] = value
            if shade is not None:
                carry = shade(value, c0[p, here, :], carry)
            return next_c, flux_x, carry

        states = []
        for i, (row, rows) in enumerate(windows):
            here = pl.ds(row, rows)
            here_c = old[first, here, :]
            flux_low = flux(wx[first - 1, here, :], old[first - 1, here, :], here_c)
            states.append((here_c, flux_low, carries[i] if carries else ()))
        return tuple(state[2] for state in sweep(first, count, unroll, body, tuple(states)))

    scale = LOG2E / (nx * views)

    def shade(value, start, carry):
        depth, through, red, green, blue = carry
        wall = start <= 0.0
        depth = depth + jnp.where(wall, 4.0, value) * scale
        after = jnp.exp2(-depth)
        weight = through - after
        shading = value / (1.0 + value)
        red = red + weight * jnp.where(wall, 0.55, shading)
        green = green + weight * jnp.where(wall, 0.5, jnp.exp2(value * (-0.5 * LOG2E)))
        blue = blue + weight * jnp.where(wall, 0.45, 0.2 + 0.6 * (shading * shading))
        return depth, after, red, green, blue

    def behind(front, back):
        depth = front[0] + back[0]
        return (depth, jnp.exp2(-depth)) + tuple(front[i] + front[1] * back[i] for i in (2, 3, 4))

    def nothing(rows):
        zero = jnp.zeros((rows, nz), jnp.float32)
        return zero, jnp.ones((rows, nz), jnp.float32), zero, zero, zero

    x0 = H + 1
    last = x0 + nx - 1
    own, middle, wide = [(Y0, ny)], [(Y0 + H, ny - 2 * H)], [(Y0 - H, ny + 2 * H)]
    along, across = near[:2], near[2:]
    for side in across:
        send_inputs(*side, 0)
    for side in along:
        send_inputs(*side)
    tell(0, near)
    for load in loads[:2]:
        load.wait()

    def mask_plane(p, carry):
        c0[p, own_rows, :] = jnp.where(b_raw[p - x0] == 0, t_raw[p - x0], 0.0)
        return carry

    sweep(x0, nx, 16, mask_plane, 0)
    for side in across:
        send_tracer(*side, 0)
    early = [copy for copy, half in sends if half == 0]
    for side in along:
        send_tracer(*side)
    for side in across:
        send_inputs(*side, 1)
        send_tracer(*side, 1)
    for load in loads[2:]:
        load.wait()
    prepare(x0, nx - 1, own, 16, "roll")
    pl.semaphore_wait(known_sem.at[0], len(near))
    if views // 2 > 2:
        tell(1, near[:2])
    for side in corners:
        send_inputs(*side)
        send_tracer(*side)
    for step in range(1, STEPS):
        advance(step, x0 + step, nx - 2 * step, own, 16, "roll")
        ring = step
        if ring < views // 2 - 1:
            pl.semaphore_wait(known_sem.at[ring], 2)
            if ring < views // 2 - 2:
                tell(ring + 1, near[:2])
    centre = advance(STEPS, x0 + H, nx - 2 * H, middle, 8, "load", shade, [nothing(ny - 2 * H)])[0]
    for i in range(5):
        mid_acc[i] = centre[i]

    for copy in early:
        copy.wait_recv()
    edges = [(Y0 - H, 2 * H), (Y0 + ny - H, 2 * H)]
    prepare(x0, split - 1, edges, 20)
    for step in range(1, STEPS):
        advance(step, x0 + step, split - 2 * step, edges, 20)
    early_edges = advance(STEPS, x0 + H, split - 2 * H, edges, 16, "load", shade, [nothing(2 * H)] * 2)
    for copy, half in sends:
        if half != 0:
            copy.wait_recv()
    prepare(1, H, wide, H)
    prepare(x0 + split - 1, nx - split + H + 1, edges, 28)
    prepare(last, H + 1, middle, H + 1)
    for step in range(1, STEPS):
        advance(step, x0 - H + step, H, wide, H)
        advance(step, x0 + split - step, nx - split + H, edges, 28)
        advance(step, x0 + nx - step, H, middle, H)
    front_edges = advance(STEPS, x0, H, edges, H, "load", shade, [nothing(2 * H)] * 2)
    edge_carries = [behind(f, b) for f, b in zip(front_edges, early_edges)]
    left, right = advance(STEPS, x0 + split - H, nx - split + H, edges, 18, "load", shade, edge_carries)
    front = advance(STEPS, x0, H, middle, H, "load", shade, [nothing(ny - 2 * H)])[0]
    centre = behind(front, [mid_acc[i] for i in range(5)])
    centre = advance(STEPS, x0 + nx - H, H, middle, H, "load", shade, [centre])[0]
    for i in range(5):
        acc[i, 0:2 * H] = left[i]
        acc[i, 2 * H:ny] = centre[i]
        acc[i, ny:ny + 2 * H] = right[i]

    store = pltpu.make_async_copy(c4.at[own_planes, own_rows], out, out_sem)
    store.start()

    stacked = jnp.concatenate([acc[i, H:H + ny] for i in (2, 3, 4, 1)], axis=0)
    part[...] = stacked.T
    share = nz // views
    copies = []
    for hop in sorted(range(1, views), key=lambda hop: -min(hop, views - hop)):
        target = lax.rem(my_view + hop, views)
        copy = pltpu.make_async_remote_copy(
            src_ref=part.at[pl.ds(pl.multiple_of(target * share, share), share)],
            dst_ref=pieces.at[my_view],
            send_sem=piece_send.at[hop - 1], recv_sem=piece_recv.at[hop - 1],
            device_id=device(hop, 0), device_id_type=MESH,
        )
        copy.start()
        copies.append(copy)
    pieces[my_view] = part[pl.ds(pl.multiple_of(my_view * share, share), share), :]
    for copy in copies:
        copy.wait_recv()
    lane = lax.broadcasted_iota(jnp.int32, (share, 4 * ny), 1)
    colors = jnp.zeros((share, 4 * ny), jnp.float32)
    through = jnp.ones((share, 4 * ny), jnp.float32)
    for brick in range(views):
        piece = pieces[brick]
        spread = piece
        for group in range(3):
            turned = pltpu.roll(piece, (group + 1) * ny, 1)
            spread = jnp.where(lane // ny == group, turned, spread)
        colors = colors + through * piece
        through = through * spread
    pixels = jnp.where(lane < 3 * ny, colors, 1.0 - through)
    for i in range(4):
        picture[i] = pixels[:, i * ny:(i + 1) * ny]

    for copy in [copy for copy, half in sends] + copies:
        copy.wait_send()
    store.wait()


def finish(tracer_next, picture, tracer_out, picture_out, sem):
    planes = tracer_next.shape[0]
    parts = 8
    each = planes // parts
    copies = [pltpu.make_async_copy(picture, picture_out, sem.at[parts])]
    for i in range(parts):
        here = pl.ds(i * each, each)
        copies.append(pltpu.make_async_copy(tracer_next.at[here], tracer_out.at[here], sem.at[i]))
    for copy in copies:
        copy.start()
    for copy in copies:
        copy.wait()


def on_device(tracer, velocity, buildings, source):
    nx, ny, nz = tracer.shape
    views, wides = lax.axis_size("view"), lax.axis_size("wide")
    field = (nx + 2 * H + 2, ny + 2 * Y0, nz)
    buffer = pltpu.VMEM(field, jnp.float32)
    n_sends = 40
    tracer_next, picture = pl.pallas_call(
        functools.partial(kernel, nx, ny, nz, views, wides, nx * 5 // 8),
        out_shape=(
            jax.ShapeDtypeStruct((nx, ny, nz), jnp.float32),
            jax.ShapeDtypeStruct((4, nz // views, ny), jnp.float32),
        ),
        in_specs=[pl.BlockSpec(memory_space=pltpu.HBM)] * 4,
        out_specs=(pl.BlockSpec(memory_space=pltpu.HBM), pl.BlockSpec(memory_space=pltpu.VMEM)),
        scratch_shapes=[
            pltpu.VMEM((nx, ny, nz), jnp.float32),
            pltpu.VMEM((3,) + field, jnp.float32),
            pltpu.VMEM((nx, ny, nz), jnp.int32),
        ]
        + [buffer] * 10
        + [
            pltpu.VMEM((5, ny + 2 * H, nz), jnp.float32),
            pltpu.VMEM((5, ny - 2 * H, nz), jnp.float32),
            pltpu.VMEM((nz, 4 * ny), jnp.float32),
            pltpu.VMEM((views, nz // views, 4 * ny), jnp.float32),
            pltpu.SemaphoreType.DMA((4,)),
            pltpu.SemaphoreType.DMA,
            pltpu.SemaphoreType.REGULAR((views // 2 - 1,)),
            pltpu.SemaphoreType.DMA((n_sends,)),
            pltpu.SemaphoreType.DMA((n_sends,)),
            pltpu.SemaphoreType.DMA((views - 1,)),
            pltpu.SemaphoreType.DMA((views - 1,)),
        ],
        compiler_params=pltpu.CompilerParams(
            collective_id=0, has_side_effects=True, vmem_limit_bytes=52 * 1024 * 1024
        ),
    )(tracer, velocity, buildings, source)
    tracer_next, picture = pl.pallas_call(
        finish,
        out_shape=(
            jax.ShapeDtypeStruct(tracer_next.shape, jnp.float32),
            jax.ShapeDtypeStruct(picture.shape, jnp.float32),
        ),
        in_specs=[pl.BlockSpec(memory_space=pl.ANY)] * 2,
        out_specs=(pl.BlockSpec(memory_space=pltpu.HBM),) * 2,
        scratch_shapes=[pltpu.SemaphoreType.DMA((9,))],
        compiler_params=pltpu.CompilerParams(vmem_limit_bytes=1024 * 1024),
    )(tracer_next, picture)
    return tracer_next, jnp.swapaxes(picture, 1, 2)


def solution(mesh):
    return jax.shard_map(
        on_device,
        mesh=mesh,
        in_specs=(
            P("view", "wide", None),
            P(None, "view", "wide", None),
            P("view", "wide", None),
            P("view", "wide", None),
        ),
        out_specs=(P("view", "wide", None), P(None, "wide", "view")),
        check_vma=False,
    )
```
